32 devices in a mesh: dp: 8 (over z, core), cp: 4 (over y, x).
Axes of the slice: x: 2, y: 2, z: 4, core: 2. Of those that a mesh axis runs over, the one named last changes fastest.
Arguments:
- tokens: bfloat16 [8, 2, 3072, 1088], P('dp', None, 'cp'), may hold values from -6 to 6
- cotangent: bfloat16 [8, 2, 3072, 1088], P('dp', None, 'cp'), may hold values from -6 to 6
- seq_lengths: int32 [8, 2, 3], P('dp'), may hold values from 1 to 2048, as said below
- block_order: int32 [8, 2, 4], P('dp'), may hold values from 0 to 3, as said below
- norm_gain: bfloat16 [2, 1088], P(None, 'dp'), may hold values from 0.5 to 1.5
- norm_shift: bfloat16 [2, 1088], P(None, 'dp'), may hold values from -1.25 to 1.25
- mix_weight: bfloat16 [1088, 3, 1088], P('dp', None, 'cp'), may hold values from -0.1875 to 0.1875
- mix_bias: bfloat16 [2, 1088], P(None, 'dp'), may hold values from -0.625 to 0.625
- out_weight: bfloat16 [1088, 1088], P('dp', 'cp'), may hold values from -1 to 1
- up_weight: bfloat16 [1088, 4352], P('dp', 'cp'), may hold values from -0.1875 to 0.1875
- up_bias: bfloat16 [4352], P('dp'), may hold values from -1.25 to 1.25
- down_weight: bfloat16 [4352, 1088], P('dp', 'cp'), may hold values from -0.09375 to 0.09375
- out_bias: bfloat16 [2, 1088], P(None, 'dp'), may hold values from -1.25 to 1.25
Outputs:
- layer_out: bfloat16 [8, 2, 3072, 1088], P('dp', None, 'cp')
- grad_tokens: bfloat16 [8, 2, 3072, 1088], P('dp', None, 'cp')
- grad_norm_gain: float32 [2, 1088], P(None, 'dp')
- grad_norm_shift: float32 [2, 1088], P(None, 'dp')
- grad_mix_weight: float32 [1088, 3, 1088], P('dp', None, 'cp')
- grad_mix_bias: float32 [2, 1088], P(None, 'dp')
- grad_out_weight: float32 [1088, 1088], P('dp', 'cp')
- grad_up_weight: float32 [1088, 4352], P('dp', 'cp')
- grad_up_bias: float32 [4352], P('dp')
- grad_down_weight: float32 [4352, 1088], P('dp', 'cp')
- grad_out_bias: float32 [2, 1088], P(None, 'dp')
The draws below stay inside these ranges and needn't reach their ends.
Inputs may be any that keep to these rules, and one draw needn't show every extreme that they name: `seq_lengths`: the 3 lengths of each pack, in order, fill its 3072 positions exactly; the longest sequence of every pack has 2048 tokens. For each pack, a permutation of the 4 blocks: device j along cp holds pack positions block_order[g, m, j] * 768 up to block_order[g, m, j] * 768 + 767.
All inputs are finite; a program needn't handle non-finite values.
Results may differ from the reference program's by a relative error of at most 0.019.
Values may be sent and summed in bfloat16 or wider, within the bound.
No kernel may reach another device: no remote copies, remote signals or barrier semaphores. Data moves between devices by JAX's collectives and lax.ppermute only.
A program may use at most 384 MiB of HBM per device.

```python
import jax
import jax.numpy as jnp
from jax import lax

D = 1088
HEADS = 17
HEAD_DIM = 64
FF = 4352
SEQ_MAX = 2048
MICRO = 2
GROUPS = 8
PACK = 3072
ROWS = 768
SEQS = 3


def single_pack(key):
    count = SEQS
    blocks = PACK // ROWS
    remain = PACK - SEQ_MAX
    key_place, key_weights, key_order, key_pick = jax.random.split(key, 4)
    longest = jax.random.randint(key_place, (), 1, count - 1)
    weights = jax.random.randint(key_weights, (count - 1,), 1, 3)
    bounds = jnp.cumsum(weights) * remain // jnp.sum(weights)
    others = bounds - jnp.concatenate((jnp.zeros((1,), jnp.int32), bounds[:-1]))
    slots = jnp.arange(count, dtype=jnp.int32)
    source = jnp.clip(jnp.where(slots < longest, slots, slots - 1), 0, count - 2)
    lengths = jnp.where(slots == longest, SEQ_MAX, others[source])
    offset = jnp.sum(jnp.where(slots < longest, lengths, 0))
    aligned = (offset % ROWS == 0).astype(jnp.int32)
    lengths = lengths - aligned * (slots == longest - 1).astype(jnp.int32) + aligned * (slots == longest + 1).astype(jnp.int32)
    offset = offset - aligned
    first = offset // ROWS
    final = (offset + SEQ_MAX - 1) // ROWS
    special = jnp.stack((first, first + 1, final))[jax.random.permutation(key_pick, 3)]
    order = jax.random.permutation(key_order, blocks)
    targets = (0, blocks // 2, blocks - 1)
    for turn in range(3):
        wanted = special[turn]
        found = jnp.argmax(order == wanted)
        displaced = order[targets[turn]]
        order = order.at[found].set(displaced).at[targets[turn]].set(wanted)
    return (lengths.astype(jnp.int32), order.astype(jnp.int32))


def pack_layout(key):
    keys = jax.random.split(key, GROUPS * MICRO)
    lengths, order = jax.vmap(single_pack)(keys)
    return (lengths.reshape(GROUPS, MICRO, SEQS), order.reshape(GROUPS, MICRO, PACK // ROWS))


def draw_seq_lengths(key, part):
    lengths, order = pack_layout(key)
    return lengths


def draw_block_order(key, part):
    lengths, order = pack_layout(key)
    return order


def shard_levels(stream_key, shape, shards, least, high):
    level = 1.0
    for dim, parts in shards:
        heights = jax.random.uniform(jax.random.fold_in(jax.random.fold_in(stream_key, 6), dim), (parts,), jnp.float32, least / len(shards), high / len(shards))
        level = level * jnp.repeat(jnp.exp(heights), shape[dim] // parts).reshape((-1,) + (1,) * (len(shape) - 1 - dim))
    return level


def normal_values(stream_key, shape, deviation, bound, cuts=(), held_as=jnp.bfloat16):
    values = jax.random.normal(stream_key, shape, jnp.float32) * deviation
    if len(cuts) > 0:
        values = shard_levels(stream_key, shape, cuts, -0.22, 0.18) * values
    return jnp.clip(values, min=-bound, max=bound).astype(held_as)


def setup_inputs(seed: int = 0) -> dict:
    seeds = jax.random.split(jax.random.key(seed), 14)
    return {
        "tokens": normal_values(seeds[0], (GROUPS, MICRO, PACK, D), 1.0, 6.0, ((0, 8), (2, 4))),
        "cotangent": normal_values(seeds[1], (GROUPS, MICRO, PACK, D), 1.0, 6.0, ((0, 8), (2, 4))),
        "seq_lengths": draw_seq_lengths(jax.random.fold_in(seeds[13], 71), 0),
        "block_order": draw_block_order(jax.random.fold_in(seeds[13], 71), 0),
        "norm_gain": jnp.clip(1.0 + 0.1 * jax.random.normal(seeds[4], (2, D), jnp.float32), 0.5, 1.5).astype(jnp.bfloat16),
        "norm_shift": normal_values(seeds[5], (2, D), 0.2, 1.25, ((1, 8),)),
        "mix_weight": normal_values(seeds[6], (D, 3, D), D ** -0.5, 0.1875, ((0, 8), (2, 4))),
        "mix_bias": normal_values(seeds[7], (2, D), 0.1, 0.625, ((1, 8),)),
        "out_weight": normal_values(seeds[8], (D, D), (D // 32) ** -0.5, 1.0, ((0, 8), (1, 4))),
        "up_weight": normal_values(seeds[9], (D, FF), D ** -0.5, 0.1875, ((0, 8), (1, 4))),
        "up_bias": normal_values(seeds[10], (FF,), 0.2, 1.25, ((0, 8),)),
        "down_weight": normal_values(seeds[11], (FF, D), FF ** -0.5, 0.09375, ((0, 8), (1, 4))),
        "out_bias": normal_values(seeds[12], (2, D), 0.2, 1.25, ((1, 8),)),
    }


EPS = 1e-05
NEG = -1e+30
HIGH = lax.Precision.HIGHEST

@jax.custom_vjp
def low(v):
    return lax.optimization_barrier(v.astype(jnp.bfloat16)).astype(jnp.float32)

@jax.custom_vjp
def low_back(v):
    return v

def low_keep(v):
    return (low(v), None)

def low_pass(kept, grad):
    return (grad,)

def back_keep(v):
    return (v, None)

def back_low(kept, grad):
    return (low(grad),)
low.defvjp(low_keep, low_pass)
low_back.defvjp(back_keep, back_low)

def layer_norm(rows, gain, shift):
    center = rows - lax.optimization_barrier(jnp.mean(rows, axis=-1, keepdims=True))
    spread = lax.optimization_barrier(jnp.mean(center * center, axis=-1, keepdims=True))
    return center * lax.rsqrt(spread + EPS) * gain + shift

def attend(query, key_rows, value_rows, places, seq_ids):
    span = min(512, PACK)
    count = PACK // span

    def block(args):
        query_block, block_places, block_seq = args
        scores = jnp.einsum('qhd,khd->qhk', query_block, key_rows, precision=HIGH) * HEAD_DIM ** (-0.5)
        scores = low_back(scores)
        allowed = (block_seq[:, None] == seq_ids[None, :]) & (places[None, :] <= block_places[:, None])
        scores = jnp.where(allowed[:, None, :], scores, NEG)
        highest = lax.optimization_barrier(jnp.max(scores, axis=-1, keepdims=True))
        weights = jnp.exp(scores - highest)
        probs = weights / lax.optimization_barrier(jnp.sum(weights, axis=-1, keepdims=True))
        return jnp.einsum('qhk,khd->qhd', low(probs), value_rows, precision=HIGH)
    result = lax.map(jax.checkpoint(block), (query.reshape(count, span, HEADS, HEAD_DIM), places.reshape(count, span), seq_ids.reshape(count, span)))
    return result.reshape(PACK, D)

def pack_forward(rows, lengths, order, params):
    gains, shifts, mix_weight, mix_bias, out_weight, up_weight, up_bias, down_weight, out_bias = params
    index = jnp.arange(PACK, dtype=jnp.int32)
    places = (order[index // ROWS] * ROWS + index % ROWS).astype(jnp.int32)
    bounds = jnp.cumsum(lengths, dtype=jnp.int32)
    seq_ids = lax.optimization_barrier(jnp.sum((places[:, None] >= bounds[None, :]).astype(jnp.int32), axis=1, dtype=jnp.int32))
    normed1 = low(layer_norm(rows, gains[0], shifts[0]))
    mixed = jnp.dot(normed1, mix_weight.reshape(D, 3 * D), precision=HIGH)
    query = low(low_back(mixed[:, :D] + mix_bias[0]))
    key_rows = low(low_back(mixed[:, D:2 * D]))
    value_rows = low(low_back(mixed[:, 2 * D:] + mix_bias[1]))
    attended = attend(query.reshape(PACK, HEADS, HEAD_DIM), key_rows.reshape(PACK, HEADS, HEAD_DIM), value_rows.reshape(PACK, HEADS, HEAD_DIM), places, seq_ids)
    attended = low(low_back(attended))
    residual = rows + low_back(jnp.dot(attended, out_weight, precision=HIGH) + out_bias[0])
    normed2 = low(layer_norm(residual, gains[1], shifts[1]))
    upper = low_back(jnp.dot(normed2, up_weight, precision=HIGH) + up_bias)
    active = low(jax.nn.gelu(upper, approximate=False))
    return residual + jnp.dot(active, down_weight, precision=HIGH) + out_bias[1]

def reference(tokens, cotangent, seq_lengths, block_order, norm_gain, norm_shift, mix_weight, mix_bias, out_weight, up_weight, up_bias, down_weight, out_bias):
    packs = GROUPS * MICRO
    inputs = tokens.astype(jnp.float32).reshape(packs, PACK, D)
    lengths = seq_lengths.reshape(packs, SEQS)
    orders = block_order.reshape(packs, PACK // ROWS)
    params = tuple((item.astype(jnp.float32) for item in (norm_gain, norm_shift, mix_weight, mix_bias, out_weight, up_weight, up_bias, down_weight, out_bias)))

    def whole(inputs, params):

        def single(args):
            return pack_forward(args[0], args[1], args[2], params)
        return lax.map(jax.checkpoint(single), (inputs, lengths, orders))
    outputs, backward = jax.vjp(whole, inputs, params)
    grad_inputs, grads = backward(cotangent.astype(jnp.float32).reshape(packs, PACK, D))
    layer_out = outputs.reshape(GROUPS, MICRO, PACK, D).astype(jnp.bfloat16)
    grad_tokens = grad_inputs.reshape(GROUPS, MICRO, PACK, D).astype(jnp.bfloat16)
    return (layer_out, grad_tokens, grads[0], grads[1], grads[2], grads[3], grads[4], grads[5], grads[6], grads[7], grads[8])
```

```python
import functools

import jax
import jax.numpy as jnp
from jax import lax
from jax.experimental.layout import Layout, with_layout_constraint
from jax.experimental import pallas as pl
from jax.experimental.pallas import tpu as pltpu
from jax.sharding import PartitionSpec as P

HEAD_DIM = 64
PAIR = 2 * HEAD_DIM
EPS = 1e-05
NEG = -1e30
TILE = 256
LOOK = 3
EXTRA = 16
VMEM_LIMIT = 56 * 1024 * 1024
UP_ROWS = 768
UP_COLS = 256
PEAK = 1.1535e15


def cost(micros, *reads):
    size = sum(item.size * item.dtype.itemsize for item in reads)
    return pl.CostEstimate(flops=int(micros * 1e-6 * PEAK), bytes_accessed=size, transcendentals=0)


def nt(a, b):
    return lax.dot_general(a, b, (((1,), (1,)), ((), ())), preferred_element_type=jnp.float32)


def nn(a, b):
    return lax.dot_general(a, b, (((1,), (0,)), ((), ())), preferred_element_type=jnp.float32)


def lanes(slot, kind):
    start = (3 * slot + kind) * PAIR
    return slice(start, start + PAIR)


def forward_kernel(tile, heads, rowat, low, mid, qkv_ref, first_ref, out_ref, lse_ref, vt_scr):
    total = qkv_ref.shape[0]
    tiles = total // tile
    slots = (heads + 1) // 2
    left = lax.broadcasted_iota(jnp.int32, (1, PAIR), 1) < HEAD_DIM

    def prepare(t, _):
        at = pl.multiple_of(rowat[t], tile)
        to = pl.multiple_of(t * tile, tile)
        for s in range(slots):
            value = qkv_ref[pl.ds(at, tile), lanes(s, 2)].astype(jnp.float32).T
            for h in range(2 * s, min(2 * s + 2, heads)):
                half = value[(h % 2) * HEAD_DIM : (h % 2 + 1) * HEAD_DIM]
                vt_scr[h, 0:HEAD_DIM, pl.ds(to, tile)] = half.astype(jnp.bfloat16)
                vt_scr[h, HEAD_DIM:, pl.ds(to, tile)] = jnp.ones((EXTRA, tile), jnp.bfloat16)
        return 0

    lax.fori_loop(0, tiles, prepare, 0)

    def query_step(t, _):
        at = pl.multiple_of(rowat[t], tile)
        to = pl.multiple_of(t * tile, tile)
        queries = []
        for s in range(slots):
            query = qkv_ref[pl.ds(at, tile), lanes(s, 0)] * jnp.asarray(HEAD_DIM**-0.5, jnp.bfloat16)
            zero = jnp.zeros_like(query)
            queries += [jnp.where(left, query, zero), jnp.where(left, zero, query)]

        def visit(masked, j, carry):
            start = pl.multiple_of(rowat[j], tile)
            there = pl.multiple_of(j * tile, tile)
            if masked:
                places = j * tile + lax.broadcasted_iota(jnp.int32, (tile, tile), 0)
                own = t * tile + lax.broadcasted_iota(jnp.int32, (tile, tile), 1)
                allowed = (places >= first_ref[0:1, pl.ds(to, tile)]) & (places <= own)
            def score(h):
                return nt(qkv_ref[pl.ds(start, tile), lanes(h // 2, 1)], queries[h])

            new = []
            ahead = [score(h) for h in range(min(LOOK, heads))]
            for h in range(heads):
                if h + LOOK < heads:
                    ahead.append(score(h + LOOK))
                top, acc = carry[2 * h], carry[2 * h + 1]
                scores = ahead[h]
                if masked:
                    scores = jnp.where(allowed, scores, NEG)
                fresh = jnp.maximum(top, jnp.max(scores, axis=0, keepdims=True))
                weights = jnp.exp(scores - fresh).astype(jnp.bfloat16)
                factor = jnp.exp(top - fresh)
                acc = acc * factor + nn(vt_scr[h, :, pl.ds(there, tile)], weights)
                new += [fresh, acc]
            return tuple(new)

        carry = (
            jnp.full((1, tile), NEG, jnp.float32),
            jnp.zeros((HEAD_DIM + EXTRA, tile), jnp.float32),
        ) * heads
        edges = mid[t] - low[t]
        carry = lax.fori_loop(mid[t], t, functools.partial(visit, False), carry)
        carry = lax.fori_loop(
            0,
            edges + 1,
            lambda i, c: visit(True, jnp.where(i < edges, low[t] + i, t), c),
            carry,
        )
        for s in range(slots):
            outs = []
            for h in (2 * s, 2 * s + 1):
                if h < heads:
                    weight_sum = carry[2 * h + 1][HEAD_DIM : HEAD_DIM + 1]
                    outs.append(carry[2 * h + 1][:HEAD_DIM] / weight_sum)
                    lse_ref[h : h + 1, pl.ds(to, tile)] = carry[2 * h] + jnp.log(weight_sum)
                else:
                    outs.append(jnp.zeros((HEAD_DIM, tile), jnp.float32))
            joined = jnp.concatenate(outs, axis=0).T
            out_ref[pl.ds(at, tile), s * PAIR : (s + 1) * PAIR] = joined.astype(out_ref.dtype)
        return 0

    lax.fori_loop(0, tiles, query_step, 0)


def attention_forward(qkv, rowat, low, mid, first, tile, heads):
    total = qkv.shape[0]
    slots = (heads + 1) // 2
    smem = pl.BlockSpec(memory_space=pltpu.SMEM)
    vmem = pl.BlockSpec(memory_space=pltpu.VMEM)
    return pl.pallas_call(
        functools.partial(forward_kernel, tile, heads),
        in_specs=[smem, smem, smem, vmem, vmem],
        out_specs=[vmem, vmem],
        out_shape=[
            jax.ShapeDtypeStruct((total, slots * PAIR), jnp.bfloat16),
            jax.ShapeDtypeStruct((heads, total), jnp.float32),
        ],
        scratch_shapes=[pltpu.VMEM((heads, HEAD_DIM + EXTRA, total), jnp.bfloat16)],
        compiler_params=pltpu.CompilerParams(vmem_limit_bytes=VMEM_LIMIT),
        cost_estimate=cost(74, qkv),
        name="attention_forward",
    )(rowat, low, mid, qkv, first)


def backward_kernel(
    tile, heads, rowat, full, high, qkv_ref, do_ref, o_ref, first_ref, lse_ref, out_ref, dq_scr, delta_scr
):
    total = qkv_ref.shape[0]
    tiles = total // tile
    slots = (heads + 1) // 2
    left = lax.broadcasted_iota(jnp.int32, (1, PAIR), 1) < HEAD_DIM
    scale = HEAD_DIM**-0.5

    def prepare(t, _):
        at = pl.multiple_of(rowat[t], tile)
        to = pl.multiple_of(t * tile, tile)
        for s in range(slots):
            part = slice(s * PAIR, (s + 1) * PAIR)
            product = do_ref[pl.ds(at, tile), part].astype(jnp.float32) * o_ref[
                pl.ds(at, tile), part
            ].astype(jnp.float32)
            flip = product.T
            for h in range(2 * s, min(2 * s + 2, heads)):
                half = flip[(h % 2) * HEAD_DIM : (h % 2 + 1) * HEAD_DIM]
                delta_scr[h : h + 1, pl.ds(to, tile)] = jnp.sum(half, axis=0, keepdims=True)
        dq_scr[:, pl.ds(to, tile)] = jnp.zeros((slots * PAIR, tile), jnp.float32)
        return 0

    lax.fori_loop(0, tiles, prepare, 0)

    def key_step(j, _):
        at = pl.multiple_of(rowat[j], tile)
        keys_t = []
        for s in range(slots):
            flip = qkv_ref[pl.ds(at, tile), lanes(s, 1)].astype(jnp.float32).T.astype(jnp.bfloat16)
            keys_t += [flip[:HEAD_DIM], flip[HEAD_DIM:]]

        def visit(masked, t, carry):
            start = pl.multiple_of(rowat[t], tile)
            to = pl.multiple_of(t * tile, tile)
            if masked:
                places = j * tile + lax.broadcasted_iota(jnp.int32, (tile, tile), 0)
                own = t * tile + lax.broadcasted_iota(jnp.int32, (tile, tile), 1)
                allowed = (places >= first_ref[0:1, pl.ds(to, tile)]) & (places <= own)
            def products(h):
                s = h // 2
                keep = left if h % 2 == 0 else ~left
                pair_query = qkv_ref[pl.ds(start, tile), lanes(s, 0)] * jnp.asarray(scale, jnp.bfloat16)
                pair_grad = do_ref[pl.ds(start, tile), s * PAIR : (s + 1) * PAIR]
                query = jnp.where(keep, pair_query, jnp.zeros_like(pair_query))
                grad = jnp.where(keep, pair_grad, jnp.zeros_like(pair_grad))
                scores = nt(qkv_ref[pl.ds(at, tile), lanes(s, 1)], query)
                grad_probs = nt(qkv_ref[pl.ds(at, tile), lanes(s, 2)], grad)
                return query, grad, scores, grad_probs

            new = list(carry)
            ahead = [products(h) for h in range(min(LOOK, heads))]
            for h in range(heads):
                if h + LOOK < heads:
                    ahead.append(products(h + LOOK))
                query, grad, scores, grad_probs = ahead[h]
                s = h // 2
                probs = jnp.exp(scores - lse_ref[h : h + 1, pl.ds(to, tile)])
                if masked:
                    probs = jnp.where(allowed, probs, 0.0)
                grad_scores = probs * (grad_probs - delta_scr[h : h + 1, pl.ds(to, tile)])
                grad_scores = grad_scores.astype(jnp.bfloat16)
                new[2 * s + 1] = new[2 * s + 1] + nn(probs.astype(jnp.bfloat16), grad)
                new[2 * s] = new[2 * s] + nn(grad_scores, query)
                here = slice(h * HEAD_DIM, (h + 1) * HEAD_DIM)
                dq_scr[here, pl.ds(to, tile)] += nn(keys_t[h], grad_scores)
            return tuple(new)

        carry = (jnp.zeros((tile, PAIR), jnp.float32),) * (2 * slots)
        carry = lax.fori_loop(j + 1, full[j], functools.partial(visit, False), carry)
        carry = lax.fori_loop(
            0,
            high[j] - full[j] + 1,
            lambda i, c: visit(True, jnp.where(i == 0, j, full[j] + i - 1), c),
            carry,
        )
        for s in range(slots):
            out_ref[pl.ds(at, tile), lanes(s, 1)] = carry[2 * s].astype(out_ref.dtype)
            out_ref[pl.ds(at, tile), lanes(s, 2)] = carry[2 * s + 1].astype(out_ref.dtype)
        return 0

    lax.fori_loop(0, tiles, key_step, 0)

    def finish(t, _):
        at = pl.multiple_of(rowat[t], tile)
        to = pl.multiple_of(t * tile, tile)
        for s in range(slots):
            grad = dq_scr[s * PAIR : (s + 1) * PAIR, pl.ds(to, tile)].T * scale
            out_ref[pl.ds(at, tile), lanes(s, 0)] = grad.astype(out_ref.dtype)
        return 0

    lax.fori_loop(0, tiles, finish, 0)


def attention_backward(qkv, grad, out, rowat, full, high, first, lse, tile, heads):
    total = qkv.shape[0]
    slots = (heads + 1) // 2
    smem = pl.BlockSpec(memory_space=pltpu.SMEM)
    vmem = pl.BlockSpec(memory_space=pltpu.VMEM)
    return pl.pallas_call(
        functools.partial(backward_kernel, tile, heads),
        in_specs=[smem, smem, smem, vmem, vmem, vmem, vmem, vmem],
        out_specs=vmem,
        out_shape=jax.ShapeDtypeStruct(qkv.shape, jnp.bfloat16),
        scratch_shapes=[
            pltpu.VMEM((slots * PAIR, total), jnp.float32),
            pltpu.VMEM((heads, total), jnp.float32),
        ],
        compiler_params=pltpu.CompilerParams(vmem_limit_bytes=VMEM_LIMIT),
        cost_estimate=cost(116, qkv),
        name="attention_backward",
    )(rowat, full, high, qkv, grad, out, first, lse)


def up_kernel(x_ref, w_ref, b_ref, active_ref, slope_ref):
    cols = w_ref.shape[2]
    cuts = [slice(at, min(at + UP_COLS, cols)) for at in range(0, cols, UP_COLS)]
    rows = x_ref[...]
    ahead = [nn(rows, w_ref[0, :, cut]) for cut in cuts[:1]]
    for k, cut in enumerate(cuts):
        if k + 1 < len(cuts):
            ahead.append(nn(rows, w_ref[0, :, cuts[k + 1]]))
        upper = ahead[k] + b_ref[0, :, cut]
        size = jnp.abs(upper)
        below = 1.0 + (0.3275911 * 0.7071067811865476) * size
        t = pl.reciprocal(below, approx=True)
        t = t * (2.0 - below * t)
        poly = 0.5 * 1.061405429
        for term in (-1.453152027, 1.421413741, -0.284496736, 0.254829592):
            poly = poly * t + 0.5 * term
        bell = jnp.exp2((upper * upper) * (-0.5 * 1.4426950408889634))
        tail = (poly * t) * bell
        normal = jnp.where(upper >= 0, 1.0 - tail, tail)
        active_ref[0, :, cut] = (upper * normal).astype(active_ref.dtype)
        slope_ref[0, :, cut] = (normal + upper * bell * 0.3989422804014327).astype(slope_ref.dtype)


def up_forward(rows, weight, bias):
    total, width = rows.shape
    slabs, _, cols = weight.shape
    span = next(size for size in (UP_ROWS, 192, 64, 16) if total % size == 0)
    out = jax.ShapeDtypeStruct((slabs, total, cols), jnp.bfloat16)
    return pl.pallas_call(
        up_kernel,
        grid=(slabs, total // span),
        in_specs=[
            pl.BlockSpec((span, width), lambda c, r: (r, 0)),
            pl.BlockSpec((1, width, cols), lambda c, r: (c, 0, 0)),
            pl.BlockSpec((1, 1, cols), lambda c, r: (c, 0, 0)),
        ],
        out_specs=[pl.BlockSpec((1, span, cols), lambda c, r: (c, r, 0))] * 2,
        out_shape=[out, out],
        compiler_params=pltpu.CompilerParams(vmem_limit_bytes=VMEM_LIMIT),
        cost_estimate=cost(30, rows, weight),
        name="up_forward",
    )(rows, weight, bias)


def norm_kernel(x_ref, gain_ref, shift_ref, out_ref):
    rows = x_ref[...].astype(jnp.float32)
    center = rows - jnp.mean(rows, axis=-1, keepdims=True)
    spread = jnp.mean(center * center, axis=-1, keepdims=True)
    rows = center * lax.rsqrt(spread + EPS) * gain_ref[...] + shift_ref[...]
    out_ref[...] = rows.astype(out_ref.dtype)


def norm_rows(rows, gain, shift):
    total, width = rows.shape
    span = next(size for size in (384, 192, 64, 16) if total % size == 0)
    vector = pl.BlockSpec((1, width), lambda r: (0, 0))
    block = pl.BlockSpec((span, width), lambda r: (r, 0))
    return pl.pallas_call(
        norm_kernel,
        grid=(total // span,),
        in_specs=[block, vector, vector],
        out_specs=block,
        out_shape=jax.ShapeDtypeStruct(rows.shape, jnp.bfloat16),
        compiler_params=pltpu.CompilerParams(vmem_limit_bytes=VMEM_LIMIT),
        cost_estimate=cost(8, rows),
        name="norm_rows",
    )(rows, gain[None], shift[None])


def merge_kernel(x_ref, out_ref):
    pieces = [x_ref[0, k].astype(jnp.float32) for k in range(x_ref.shape[1])]
    out_ref[0] = jnp.concatenate(pieces, axis=1).astype(out_ref.dtype)


def merge_lanes(values):
    slabs, pieces, rows, cols = values.shape
    if pieces == 1:
        return values[:, 0]
    span = next(size for size in (272, 64, 16, rows) if rows % size == 0)
    return pl.pallas_call(
        merge_kernel,
        grid=(slabs, rows // span),
        in_specs=[pl.BlockSpec((1, pieces, span, cols), lambda c, r: (c, 0, r, 0))],
        out_specs=pl.BlockSpec((1, span, pieces * cols), lambda c, r: (c, r, 0)),
        out_shape=jax.ShapeDtypeStruct((slabs, rows, pieces * cols), values.dtype),
        compiler_params=pltpu.CompilerParams(vmem_limit_bytes=VMEM_LIMIT),
        cost_estimate=cost(8, values),
        name="merge_lanes",
    )(values)


def pack_lanes(columns):
    cols = columns[0].shape[1]
    whole = cols // PAIR * PAIR
    pieces = [item[:, at : at + PAIR] for item in columns for at in range(0, whole, PAIR)]
    if cols > whole:
        rest = jnp.concatenate([item[:, whole:] for item in columns], axis=1)
        spare = -rest.shape[1] % PAIR
        rest = jnp.concatenate((rest, jnp.zeros((rest.shape[0], spare), rest.dtype)), axis=1)
        pieces += [rest[:, at : at + PAIR] for at in range(0, rest.shape[1], PAIR)]
    return pieces


def unpack_lanes(pieces, cols):
    count = cols // PAIR
    left = cols - count * PAIR
    rest = jnp.concatenate(pieces[3 * count :], axis=1) if left else None
    return [
        jnp.concatenate(
            list(pieces[k * count : (k + 1) * count]) + ([rest[:, k * left : (k + 1) * left]] if left else []),
            axis=1,
        )
        for k in range(3)
    ]


def mix_take_kernel(main, parts, cols, part_ref, x_ref, out_ref):
    part = part_ref[0]
    slots = main // PAIR
    shards = [
        unpack_lanes([x_ref[c, 0, k].astype(jnp.float32) for k in range(x_ref.shape[2])], cols)
        for c in range(x_ref.shape[0])
    ]
    for kind in range(3):
        full = jnp.concatenate([shard[kind] for shard in shards], axis=1)
        own = full[:, :main]
        for k in range(1, parts):
            own = jnp.where(part == k, full[:, k * main : (k + 1) * main], own)
        last = full[:, parts * main :]
        last = jnp.where(part == 0, last, 0.0)
        last = jnp.concatenate((last, jnp.zeros_like(last)), axis=1)
        for s in range(slots + 1):
            piece = own[:, s * PAIR : (s + 1) * PAIR] if s < slots else last
            out_ref[0, :, lanes(s, kind)] = piece.astype(out_ref.dtype)


def mix_take(shards, part, main, parts, cols):
    ncp, ndp, pieces, rows, _ = shards.shape
    width = 3 * (main + PAIR)
    return pl.pallas_call(
        functools.partial(mix_take_kernel, main, parts, cols),
        grid=(ndp,),
        in_specs=[
            pl.BlockSpec(memory_space=pltpu.SMEM),
            pl.BlockSpec((ncp, 1, pieces, rows, PAIR), lambda d: (0, d, 0, 0, 0)),
        ],
        out_specs=pl.BlockSpec((1, rows, width), lambda d: (d, 0, 0)),
        out_shape=jax.ShapeDtypeStruct((ndp, rows, width), shards.dtype),
        compiler_params=pltpu.CompilerParams(vmem_limit_bytes=VMEM_LIMIT),
        cost_estimate=cost(8, shards),
        name="mix_take",
    )(part.reshape(1), shards)


def mix_spread_kernel(main, parts, cols, at_ref, x_ref, keep_ref, send_ref):
    part, core = at_ref[0], at_ref[1]
    slots = main // PAIR
    for out_ref, row in ((keep_ref, core), (send_ref, 1 - core)):
        kinds = []
        for kind in range(3):
            pieces = [x_ref[row, :, lanes(s, kind)].astype(jnp.float32) for s in range(slots + 1)]
            own = jnp.concatenate(pieces[:slots], axis=1)
            last = pieces[slots][:, :HEAD_DIM]
            full = [jnp.where(part == k, own, 0.0) for k in range(parts)]
            full.append(jnp.where(part == 0, last, 0.0))
            kinds.append(jnp.concatenate(full, axis=1))
        for c in range(out_ref.shape[1]):
            packed = pack_lanes([full[:, c * cols : (c + 1) * cols] for full in kinds])
            for k, piece in enumerate(packed):
                out_ref[0, c, k] = piece.astype(out_ref.dtype)


def mix_spread(grad, part, core, main, parts, ncp):
    ndp, rows, width = grad.shape
    cols = (parts * main + HEAD_DIM) // ncp
    pieces = 3 * (cols // PAIR) + -(-3 * (cols % PAIR) // PAIR)
    out = jax.ShapeDtypeStruct((ndp // 2, ncp, pieces, rows, PAIR), grad.dtype)
    return pl.pallas_call(
        functools.partial(mix_spread_kernel, main, parts, cols),
        grid=(ndp // 2,),
        in_specs=[
            pl.BlockSpec(memory_space=pltpu.SMEM),
            pl.BlockSpec((2, rows, width), lambda d: (d, 0, 0)),
        ],
        out_specs=[pl.BlockSpec((1, ncp, pieces, rows, PAIR), lambda d: (d, 0, 0, 0, 0))] * 2,
        out_shape=[out, out],
        compiler_params=pltpu.CompilerParams(vmem_limit_bytes=VMEM_LIMIT),
        cost_estimate=cost(8, grad),
        name="mix_spread",
    )(jnp.stack((part, core)), grad)


def pack_tables(order_row, lengths, rows, tile):
    blocks = order_row.shape[0]
    total = blocks * rows
    tiles = total // tile
    places = jnp.arange(total, dtype=jnp.int32)
    ends = jnp.cumsum(lengths, dtype=jnp.int32)
    begins = ends - lengths
    seq = jnp.sum((places[:, None] >= ends[None, :]).astype(jnp.int32), axis=1)
    pick = seq[:, None] == jnp.arange(lengths.shape[0], dtype=jnp.int32)[None, :]
    first = jnp.sum(jnp.where(pick, begins[None, :], 0), axis=1)
    last = jnp.sum(jnp.where(pick, ends[None, :], 0), axis=1) - 1
    index = jnp.arange(tiles, dtype=jnp.int32)
    per = rows // tile
    holder = holders(order_row)
    slots = jnp.arange(blocks, dtype=jnp.int32)
    held = (index // per)[:, None] == slots[None, :]
    rowat = jnp.sum(jnp.where(held, holder[None, :], 0), axis=1) * rows + (index % per) * tile
    firsts = first.reshape(tiles, tile)
    lasts = last.reshape(tiles, tile)
    low = firsts[:, 0] // tile
    mid = jnp.minimum((firsts[:, -1] + tile - 1) // tile, index)
    high = lasts[:, -1] // tile + 1
    full = jnp.clip((lasts[:, 0] + 1) // tile, index + 1, high)
    return rowat, low, mid, full, high, first[None]


def holders(order_row):
    slots = jnp.arange(order_row.shape[0], dtype=jnp.int32)
    return jnp.sum(
        jnp.where(order_row[None, :] == slots[:, None], slots[None, :], 0), axis=1, dtype=jnp.int32
    )


def low(values):
    return values.astype(jnp.bfloat16)


def wide(values):
    return values.astype(jnp.float32)


def row_major(values):
    return with_layout_constraint(values, Layout(tuple(range(values.ndim))))


def normalize(rows):
    center = rows - jnp.mean(rows, axis=-1, keepdims=True)
    rstd = lax.rsqrt(jnp.mean(center * center, axis=-1, keepdims=True) + EPS)
    return center * rstd, rstd


def normalize_back(grad, gain, xhat, rstd):
    scaled = grad * gain
    mean = jnp.mean(scaled, axis=-1, keepdims=True)
    slope = jnp.mean(scaled * xhat, axis=-1, keepdims=True)
    return rstd * (scaled - mean - xhat * slope)


def flip_bit(values, axis, place):
    return lax.ppermute(values, axis, [(i, i ^ (1 << place)) for i in range(lax.axis_size(axis))])


def halve(values, bits, bit):
    at = bits.index(bit)
    axis, place = bit
    own = (lax.axis_index(axis) >> place) & 1
    send = lax.dynamic_index_in_dim(values, 1 - own, at, keepdims=False)
    keep = lax.dynamic_index_in_dim(values, own, at, keepdims=False)
    got = flip_bit(send, axis, place)
    return (wide(keep) + wide(got)).astype(values.dtype), bits[:at] + bits[at + 1 :]


def bits_of(axis):
    return tuple((axis, place) for place in reversed(range(lax.axis_size(axis).bit_length() - 1)))


def split_bits(values, lead, bits):
    return values.reshape((2,) * len(bits) + values.shape[lead:])


def tie(*values):
    return lax.optimization_barrier(values)


def begin(values, bits):
    cut = min((values.shape[-2] // 2 + 7) // 8 * 8, values.shape[-2])
    near = sorted(bit for bit in bits if bit[0] == "cp")
    far = sorted(bit for bit in bits if bit[0] == "dp")
    halves = (values[..., :cut, :], near + far), (values[..., cut:, :], near[::-1] + far)
    return [(piece, bits, order) for piece, order in halves if piece.shape[-2]]


def step(state):
    done = []
    for piece, left, order in state:
        if order:
            piece, left = halve(piece, left, order[0])
        done.append((piece, left, order[1:]))
    return done


def held(state):
    return [piece for piece, _, _ in state]


def placed(state, pieces):
    return [(piece,) + item[1:] for piece, item in zip(pieces, state)]


def finish(state):
    while any(order for _, _, order in state):
        state = step(state)
    return wide(jnp.concatenate(held(state), axis=-2))


def flip_role(values, place):
    ndp, ncp = lax.axis_size("dp"), lax.axis_size("cp")
    pairs = []
    for d in range(ndp):
        bit = 1 << (place if d % 2 == 0 else 1 - place)
        pairs += [(d * ncp + c, d * ncp + (c ^ bit)) for c in range(ncp)]
    return lax.ppermute(values, ("dp", "cp"), pairs)


def role_of(index):
    swapped = (index >> 1) | ((index & 1) << 1)
    return jnp.where(lax.axis_index("dp") % 2 == 0, index, swapped)


def gather_pack(values, mine, crossed):
    own = lax.dynamic_index_in_dim(values, mine, 0, keepdims=False)
    if crossed:
        other = lax.dynamic_index_in_dim(values, 1 - mine, 0, keepdims=False)
        beside = flip_role(own, 0)
        below = flip_role(other, 1)
        return jnp.stack((own, beside, below, flip_role(below, 0)))
    whole = lax.all_gather(values, "cp", axis=0)
    return lax.dynamic_index_in_dim(whole, mine, 1, keepdims=False)


def scatter_pack(values, mine, micro, crossed):
    if crossed:
        own = low(wide(values[0]) + wide(flip_role(values[1], 0)))
        below = low(wide(values[2]) + wide(flip_role(values[3], 0)))
        other = flip_role(below, 1)
        first = mine == 0
        return jnp.stack((jnp.where(first, own, other), jnp.where(first, other, own)))
    slots = jnp.arange(micro, dtype=jnp.int32)
    spread = jnp.where((slots == mine)[None, :, None, None], values[:, None], jnp.zeros((), values.dtype))
    return lax.psum_scatter(spread, "cp", scatter_dimension=0, tiled=False)


def heads_to_rows(values, mine, part, micro, parts, crossed):
    _, rows, width = values.shape
    if crossed:
        got = (
            values[0],
            flip_role(values[1], 0),
            flip_role(values[2], 1),
            lax.ppermute(values[3], "cp", [(i, i ^ 3) for i in range(4)]),
        )
        first = part == 0
        pair = [
            jnp.concatenate((jnp.where(first, a, b), jnp.where(first, b, a)), axis=1)
            for a, b in ((got[0], got[1]), (got[2], got[3]))
        ]
        first = mine == 0
        return jnp.stack((jnp.where(first, pair[0], pair[1]), jnp.where(first, pair[1], pair[0])))
    got = lax.all_to_all(values, "cp", 0, 0, tiled=True).reshape(micro, parts, rows, width)
    return got.transpose(0, 2, 1, 3).reshape(micro, rows, parts * width)


def rows_to_heads(values, mine, part, micro, parts, crossed):
    _, rows, width = values.shape
    width = width // parts
    if crossed:
        first = mine == 0
        own = jnp.where(first, values[0], values[1])
        other = jnp.where(first, values[1], values[0])
        first = part == 0
        pieces = []
        for item in (own, other):
            a, b = item[:, :width], item[:, width:]
            pieces += [jnp.where(first, a, b), jnp.where(first, b, a)]
        return jnp.stack((
            pieces[0],
            flip_role(pieces[1], 0),
            flip_role(pieces[2], 1),
            lax.ppermute(pieces[3], "cp", [(i, i ^ 3) for i in range(4)]),
        ))
    cut = values.reshape(micro, rows, parts, width).transpose(0, 2, 1, 3)
    return lax.all_to_all(cut.reshape(micro * parts, rows, width), "cp", 0, 0, tiled=True)


def per_device(
    tokens,
    cotangent,
    seq_lengths,
    block_order,
    norm_gain,
    norm_shift,
    mix_weight,
    mix_bias,
    out_weight,
    up_weight,
    up_bias,
    down_weight,
    out_bias,
):
    micro, rows, width = tokens.shape[1:]
    ndp, ncp = lax.axis_size("dp"), lax.axis_size("cp")
    device = lax.axis_index("cp")
    parts = ncp // micro
    crossed = ncp == 4 and micro == 2 and rows % TILE == 0
    role = role_of(device) if crossed else device
    mine, part = role // parts, role % parts
    core_index = lax.axis_index("dp") % 2
    heads = width // HEAD_DIM
    per = heads // 2 // parts
    slots = per + 1
    own_heads = 2 * per + 1
    main = per * PAIR
    odd = width - HEAD_DIM
    ff = down_weight.shape[0] * ndp
    cells = width // ndp
    count = micro * rows
    total = ncp * rows

    def gather(shard, axes):
        return lax.all_gather(shard, axes, axis=0, tiled=False)

    tokens = row_major(tokens)
    cotangent = row_major(cotangent)
    small = jnp.concatenate(
        [item.reshape(1, -1) for item in (norm_gain, norm_shift, mix_bias, out_bias, up_bias)],
        axis=1,
    )
    small = wide(lax.all_gather(small, "dp", axis=0, tiled=True))
    gains, shifts, mix_biases, out_biases = (
        small[:, k * 2 * cells : (k + 1) * 2 * cells]
        .reshape(ndp, 2, cells)
        .transpose(1, 0, 2)
        .reshape(2, width)
        for k in range(4)
    )
    up_biases = small[:, 8 * cells :].reshape(-1)

    pack = gather_pack(tokens[0], mine, crossed)
    mix_all = gather(
        jnp.stack(pack_lanes([mix_weight[:, k] for k in range(3)])), ("cp", "dp")
    )
    out_all = gather(out_weight, ("cp", "dp"))
    up_all = gather(up_weight, ("cp", "dp"))
    down_all = gather(down_weight.T, ("dp", "cp"))
    mix_own = mix_take(
        mix_all.reshape((ncp, ndp) + mix_all.shape[1:]), part, main, parts, width // ncp
    )
    mix_own = mix_own.reshape(width, -1)
    out_full = merge_lanes(out_all.reshape(1, ncp, width, -1))[0]
    up_slabs = up_all.reshape(ncp, width, ff // ncp)
    down_slabs = merge_lanes(down_all.reshape(ncp, ndp // ncp, width, -1))

    def own_columns(values):
        head = lax.dynamic_slice_in_dim(values, part * main, main, values.ndim - 1)
        last = jnp.where(part == 0, values[..., odd:], jnp.zeros((), values.dtype))
        return jnp.concatenate((head, last, jnp.zeros_like(last)), axis=-1)

    def from_own_columns(values):
        blank = jnp.zeros(values.shape[:-1] + (odd,), values.dtype)
        last = jnp.where(part == 0, values[..., main : main + HEAD_DIM], jnp.zeros((), values.dtype))
        spread = lax.dynamic_update_slice_in_dim(blank, values[..., :main], part * main, values.ndim - 1)
        return jnp.concatenate((spread, last), axis=-1)

    def slot_major(values):
        lead = values.shape[:-2]
        cut = values.reshape(lead + (3, slots, PAIR))
        return jnp.swapaxes(cut, -3, -2).reshape(lead + (slots * 3 * PAIR,))

    def kind_major(values):
        lead = values.shape[:-1]
        cut = values.reshape(lead + (slots, 3, PAIR))
        return jnp.swapaxes(cut, -3, -2).reshape(lead + (3, slots * PAIR))

    order_row = lax.dynamic_index_in_dim(block_order[0], mine, 0, keepdims=False)
    lengths = lax.dynamic_index_in_dim(seq_lengths[0], mine, 0, keepdims=False)
    places = jnp.arange(ncp, dtype=jnp.int32)
    if crossed:
        relative = places[:, None] == role_of(places ^ role)[None, :]
        kept_order = jnp.sum(jnp.where(relative, order_row[:, None], 0), axis=0, dtype=jnp.int32)
        tables = pack_tables(kept_order, lengths, rows, TILE)
    else:
        pack = jnp.take(pack, holders(order_row), axis=0)
        tables = pack_tables(jnp.zeros((1,), jnp.int32), lengths, total, TILE)
    rowat, tile_low, tile_mid, tile_full, tile_high, first = tables

    def to_devices(values):
        values = values.reshape(ncp, rows, -1)
        return values if crossed else jnp.take(values, order_row, axis=0)

    def to_places(values):
        values = values if crossed else jnp.take(values, holders(order_row), axis=0)
        return values.reshape(total, -1)

    pack, mix_own = tie(pack, mix_own)
    pack_low = norm_rows(pack.reshape(total, width), gains[0], shifts[0])
    bias_own = slot_major(
        own_columns(jnp.stack((mix_biases[0], jnp.zeros((width,), jnp.float32), mix_biases[1])))
    )
    mixed = low(jnp.dot(pack_low, mix_own, preferred_element_type=jnp.float32) + bias_own)
    attended_own, log_sums = attention_forward(
        mixed, rowat, tile_low, tile_mid, first, TILE, own_heads
    )
    attended = heads_to_rows(to_devices(attended_own), mine, part, micro, parts, crossed)
    attended = attended.reshape(count, parts * slots * PAIR)

    pieces = []
    for k in range(parts):
        pieces.append(out_full[k * main : (k + 1) * main])
        last = out_full[odd:] if k == 0 else jnp.zeros((HEAD_DIM, width), jnp.bfloat16)
        pieces += [last, jnp.zeros((HEAD_DIM, width), jnp.bfloat16)]
    out_own = jnp.concatenate(pieces, axis=0)

    source = wide(tokens[0].reshape(count, width))
    residual = (
        source + jnp.dot(attended, out_own, preferred_element_type=jnp.float32) + out_biases[0]
    )
    hat2, rstd2 = normalize(residual)
    normed2 = low(hat2 * gains[1] + shifts[1])
    active, slope = up_forward(normed2, up_slabs, up_biases.reshape(ncp, 1, ff // ncp))
    result = (
        residual
        + jnp.einsum("ctf,cdf->td", active, down_slabs, preferred_element_type=jnp.float32)
        + out_biases[1]
    )
    layer_out = low(result).reshape(1, micro, rows, width)

    dp_bits, cp_bits = bits_of("dp"), bits_of("cp")
    core = ("dp", 0)
    grad_out = cotangent[0].reshape(count, width)
    grad_down = low(jnp.einsum("td,ctf->cdf", grad_out, active, preferred_element_type=jnp.float32))
    grad_down, grad_out = tie(grad_down, grad_out)
    if ndp == 2 * ncp:
        half = ff // ndp
        own = core_index == 0
        near, far = grad_down[..., :half], grad_down[..., half:]
        got = flip_bit(jnp.where(own, far, near), "dp", 0)
        down_sum = low(wide(jnp.where(own, near, far)) + wide(got))
        down_left = dp_bits[:-1] + cp_bits
        down_sum = split_bits(down_sum.reshape(ncp, ncp, -1, half), 2, down_left)
    else:
        down_sum = split_bits(grad_down.reshape(ndp, ncp, -1, ff // ndp), 2, dp_bits + cp_bits)
        down_sum, down_left = halve(down_sum, dp_bits + cp_bits, core)
    grad_active = jnp.einsum("td,cdf->ctf", grad_out, down_slabs, preferred_element_type=jnp.float32)
    grad_upper = low(grad_active * wide(slope))
    grad_upper, down_sum = tie(grad_upper, down_sum)
    grad_up = low(jnp.einsum("td,ctf->cdf", normed2, grad_upper, preferred_element_type=jnp.float32))
    grad_up, grad_upper = tie(grad_up, grad_upper)
    up_sum = split_bits(grad_up.reshape(ncp, ndp, cells, -1), 2, cp_bits + dp_bits)
    up_sum, up_left = halve(up_sum, cp_bits + dp_bits, core)
    down_state = step(begin(down_sum, down_left))
    grad_normed2 = jnp.einsum(
        "ctf,cdf->td", grad_upper, up_slabs, preferred_element_type=jnp.float32
    )
    grad_normed2, up_sum, *pieces = tie(grad_normed2, up_sum, *held(down_state))
    down_state = step(placed(down_state, pieces))
    grad_residual = wide(grad_out) + normalize_back(grad_normed2, gains[1], hat2, rstd2)
    grad_branch = low(grad_residual)
    grad_attended = low(
        jnp.einsum("td,ed->te", grad_branch, out_own, preferred_element_type=jnp.float32)
    )
    grad_attended, grad_branch, *pieces = tie(grad_attended, grad_branch, *held(down_state))
    down_state = placed(down_state, pieces)
    grad_attended = rows_to_heads(
        grad_attended.reshape(micro, rows, -1), mine, part, micro, parts, crossed
    )
    grad_proj = low(
        jnp.einsum("te,td->ed", attended, grad_branch, preferred_element_type=jnp.float32)
    )
    stride = slots * PAIR
    grad_proj = jnp.concatenate(
        [grad_proj[k * stride : k * stride + main] for k in range(parts)]
        + [grad_proj[main : main + HEAD_DIM]],
        axis=0,
    )
    proj_sum = split_bits(grad_proj.reshape(ndp, cells, width), 1, dp_bits)
    proj_sum, proj_left = halve(proj_sum, dp_bits, core)
    lead = len(proj_left)
    proj_sum = jnp.moveaxis(proj_sum.reshape(proj_sum.shape[:-1] + (ncp, -1)), -2, lead)
    proj_sum = proj_sum.reshape((2,) * (lead + len(cp_bits)) + proj_sum.shape[lead + 1 :])
    proj_left = proj_left + cp_bits

    grad_attended, layer_out, up_sum, proj_sum, *pieces = tie(
        grad_attended, layer_out, up_sum, proj_sum, *held(down_state)
    )
    down_state = step(placed(down_state, pieces))
    up_state = step(begin(up_sum, up_left))
    proj_state = step(begin(proj_sum, proj_left))
    grad_mixed = attention_backward(
        mixed,
        to_places(grad_attended),
        attended_own,
        rowat,
        tile_full,
        tile_high,
        first,
        log_sums,
        TILE,
        own_heads,
    )
    states = (down_state, up_state, proj_state)
    grad_mixed, *pieces = tie(grad_mixed, *[piece for state in states for piece in held(state)])
    down_state, up_state, proj_state = (
        placed(state, [pieces.pop(0) for _ in state]) for state in states
    )
    grad_normed1 = low(
        jnp.einsum("te,de->td", grad_mixed, mix_own, preferred_element_type=jnp.float32)
    )
    grad_normed1, grad_mixed = tie(grad_normed1, grad_mixed)
    grad_normed1 = wide(
        scatter_pack(to_devices(grad_normed1), mine, micro, crossed).reshape(count, width)
    )
    grad_mix = jnp.einsum("td,te->de", pack_low, grad_mixed, preferred_element_type=jnp.float32)
    keep, send = mix_spread(
        low(grad_mix).reshape(ndp, cells, -1), part, core_index, main, parts, ncp
    )
    mix_sum = low(wide(keep) + wide(flip_bit(send, "dp", 0)))
    mix_bits = dp_bits[:-1] + cp_bits
    mix_sum = mix_sum.reshape((2,) * len(mix_bits) + (-1, PAIR))
    grad_mix_own = finish(begin(mix_sum, mix_bits)).reshape(-1, cells, PAIR)
    grad_mix_own = jnp.stack(unpack_lanes(list(grad_mix_own), width // ncp), axis=1)
    mixed_sums = from_own_columns(kind_major(jnp.sum(wide(grad_mixed), axis=0)))
    grad_down_own = finish(down_state).T
    grad_up_own = finish(up_state)
    grad_proj_own = finish(proj_state)

    hat1, rstd1 = normalize(source)
    grad_tokens = grad_residual + normalize_back(grad_normed1, gains[0], hat1, rstd1)
    grad_tokens = low(grad_tokens).reshape(1, micro, rows, width)

    vectors = (
        jnp.stack((jnp.sum(grad_normed1 * hat1, axis=0), jnp.sum(grad_normed2 * hat2, axis=0))),
        jnp.stack((jnp.sum(grad_normed1, axis=0), jnp.sum(grad_normed2, axis=0))),
        jnp.stack((mixed_sums[0], mixed_sums[2])),
        jnp.stack((jnp.sum(wide(grad_branch), axis=0), jnp.sum(wide(grad_out), axis=0))),
    )
    flat = [item.reshape(2, ndp, cells).transpose(1, 0, 2).reshape(ndp, -1) for item in vectors]
    flat.append(jnp.sum(wide(grad_upper), axis=1).reshape(ndp, -1))
    flat = split_bits(jnp.concatenate(flat, axis=1), 1, dp_bits)
    left = dp_bits
    for bit in sorted(dp_bits):
        flat, left = halve(flat, left, bit)
    for axis, place in sorted(cp_bits):
        flat = flat + flip_bit(flat, axis, place)
    sums = flat
    parts_out = [sums[k * 2 * cells : (k + 1) * 2 * cells].reshape(2, cells) for k in range(4)]
    grad_upb = sums[8 * cells :]
    return (
        layer_out,
        grad_tokens,
        parts_out[0],
        parts_out[1],
        grad_mix_own,
        parts_out[2],
        grad_proj_own,
        grad_up_own,
        grad_upb,
        grad_down_own,
        parts_out[3],
    )


def solution(mesh):
    placed = (
        P("dp", None, "cp", None),
        P("dp", None, "cp", None),
        P("dp", None, None),
        P("dp", None, None),
        P(None, "dp"),
        P(None, "dp"),
        P("dp", None, "cp"),
        P(None, "dp"),
        P("dp", "cp"),
        P("dp", "cp"),
        P("dp"),
        P("dp", "cp"),
        P(None, "dp"),
    )
    return jax.shard_map(
        per_device,
        mesh=mesh,
        in_specs=placed,
        out_specs=(
            P("dp", None, "cp", None),
            P("dp", None, "cp", None),
            P(None, "dp"),
            P(None, "dp"),
            P("dp", None, "cp"),
            P(None, "dp"),
            P("dp", "cp"),
            P("dp", "cp"),
            P("dp"),
            P("dp", "cp"),
            P(None, "dp"),
        ),
        check_vma=False,
    )
```
